256 devices in a mesh: dp: 8 (over y, x_lo), ctx: 32 (over x_hi, z, core).
Axes of the slice: x: 4 (x_hi: 2, x_lo: 2; x = x_hi * 2 + x_lo), y: 4, z: 8, core: 2. Of those that a mesh axis runs over, the one named last changes fastest.
Arguments:
- tokens: bfloat16 [8, 8192, 5120], P('dp', 'ctx'), as said below
- queries: bfloat16 [8, 8192, 2560], P('dp', 'ctx'), as said below
- norm_gain: bfloat16 [5120], replicated, may hold values from 0.5 to 1.5
- key_weight: bfloat16 [5120, 512], P('dp'), may hold values from -0.078125 to 0.078125
- value_weight: bfloat16 [5120, 512], P('dp'), may hold values from -0.078125 to 0.078125
Outputs:
- attended: bfloat16 [8, 8192, 2560], P('dp', 'ctx')
The draws below stay inside these ranges and needn't reach their ends.
Inputs may be any that keep to these rules, and one draw needn't show every extreme that they name: `tokens`: hidden states of a position and feature. Projected queries.
All inputs are finite; a program needn't handle non-finite values.
Results may differ from the reference program's by a relative error of at most 0.0099.
Values may be sent and summed in bfloat16 or wider, within the bound.
No kernel may reach another device: no remote copies, remote signals or barrier semaphores. Data moves between devices by JAX's collectives and lax.ppermute only.
A program may use at most 128 MiB of HBM per device.

```python
import math
import jax
import jax.numpy as jnp
from jax import lax

D = 5120
KVH = 4
GROUP = 5
HD = 128
SEQ = 8192
SEQS = 8


def draw_tokens(key, part):
    key = jax.random.fold_in(key, 11)
    key_base, key_rows, key_cols = jax.random.split(key, 3)
    array_shape = (SEQS, SEQ, D)
    base = jnp.clip(jax.random.normal(key_base, array_shape, jnp.float32), -6.0, 6.0)
    row_scale = jnp.exp(jax.random.uniform(key_rows, (SEQS, SEQ, 1), jnp.float32, 0.0, math.log(10.0)))
    column_scale = jnp.exp(jax.random.uniform(key_cols, (1, 1, D), jnp.float32, math.log(0.3), math.log(3.0)))
    return (base * row_scale * column_scale).astype(jnp.bfloat16)


def draw_queries(key, part):
    key = jax.random.fold_in(key, 12)
    key_base = jax.random.fold_in(key, 0)
    array_shape = (SEQS, SEQ, KVH * GROUP * HD)
    base = 2.5 * jnp.clip(jax.random.normal(key_base, array_shape, jnp.float32), -6.0, 6.0)
    return base.astype(jnp.bfloat16)


def shard_levels(stream_key, dims, cuts, low, largest):
    def one(axis_at, blocks):
        draws = jax.random.uniform(jax.random.fold_in(jax.random.fold_in(stream_key, 6), axis_at), (blocks,), jnp.float32, low / len(cuts), largest / len(cuts))
        return jnp.repeat(jnp.exp(draws), dims[axis_at] // blocks).reshape((-1,) + (1,) * (len(dims) - axis_at - 1))

    loudness = one(*cuts[0])
    for cut in cuts[1:]:
        loudness = loudness * one(*cut)
    return loudness


def gaussian(rng, shape, scale, limit, shards=(), kind=jnp.bfloat16):
    values = scale * jax.random.normal(rng, shape, jnp.float32)
    if shards:
        values = values * shard_levels(rng, shape, shards, -0.22, 0.18)
    return jnp.clip(values, -limit, limit).astype(kind)


def setup_inputs(seed: int = 0) -> dict:
    streams_of = jax.random.split(jax.random.key(seed), 6)
    tokens = draw_tokens(jax.random.fold_in(streams_of[5], 71), 0)
    queries = draw_queries(jax.random.fold_in(streams_of[5], 71), 0)
    norm_gain = jnp.clip(1.0 + 0.1 * jax.random.normal(streams_of[2], (D,), jnp.float32), 0.5, 1.5).astype(jnp.bfloat16)
    key_weight = gaussian(streams_of[3], (D, KVH * HD), D ** -0.5, 0.078125, ((0, 8),))
    value_weight = gaussian(streams_of[4], (D, KVH * HD), D ** -0.5, 0.078125, ((0, 8),))
    return dict(tokens=tokens, queries=queries, norm_gain=norm_gain, key_weight=key_weight, value_weight=value_weight)


def reference(tokens, queries, norm_gain, key_weight, value_weight):
    values32 = tokens.astype(jnp.float32)
    mean_square = lax.optimization_barrier(jnp.mean(values32 * values32, axis=-1, keepdims=True))
    normed = (values32 * lax.rsqrt(mean_square + 1e-05) * norm_gain.astype(jnp.float32)).astype(jnp.bfloat16)
    normed = normed.reshape(SEQS * SEQ, D)
    key_rows = jnp.dot(normed, key_weight, preferred_element_type=jnp.float32).astype(jnp.bfloat16)
    value_rows = jnp.dot(normed, value_weight, preferred_element_type=jnp.float32).astype(jnp.bfloat16)
    key_rows = key_rows.reshape(SEQS, SEQ, KVH, HD)
    value_rows = value_rows.reshape(SEQS, SEQ, KVH, HD)
    block_rows = min(512, SEQ)
    query_blocks = queries.reshape(SEQS, SEQ // block_rows, block_rows, KVH, GROUP, HD)

    def per_sequence(sequence_index):
        keys_here = key_rows[sequence_index].astype(jnp.float32)
        values_here = value_rows[sequence_index].astype(jnp.float32)
        blocks_here = query_blocks[sequence_index]

        def per_block(block_index):
            query_here = blocks_here[block_index].astype(jnp.float32)
            scores = jnp.einsum('tkgd,skd->tkgs', query_here, keys_here, precision=lax.Precision.HIGHEST) * HD ** (-0.5)
            query_pos = block_index * block_rows + lax.iota(jnp.int32, block_rows)
            key_pos = lax.iota(jnp.int32, SEQ)
            allowed = (key_pos[None, :] <= query_pos[:, None])[:, None, None, :]
            scores = jnp.where(allowed, scores, -jnp.inf)
            row_max = lax.optimization_barrier(jnp.max(scores, axis=-1, keepdims=True))
            weights = jnp.where(allowed, jnp.exp(scores - row_max), 0.0)
            total = lax.optimization_barrier(jnp.sum(weights, axis=-1))
            low_weights = weights.astype(jnp.bfloat16).astype(jnp.float32)
            summed = jnp.einsum('tkgs,skd->tkgd', low_weights, values_here, precision=lax.Precision.HIGHEST)
            result = summed / total[..., None]
            return result.astype(jnp.bfloat16).reshape(block_rows, KVH * GROUP * HD)
        outputs = lax.map(per_block, jnp.arange(SEQ // block_rows, dtype=jnp.int32))
        return outputs.reshape(SEQ, KVH * GROUP * HD)
    return lax.map(per_sequence, jnp.arange(SEQS, dtype=jnp.int32))
```

```python
import functools

import jax
import jax.numpy as jnp
from jax import lax
from jax.experimental import pallas as pl
from jax.experimental.pallas import tpu as pltpu
from jax.sharding import Mesh
from jax.sharding import PartitionSpec as P

GROUP = 5
HD = 128
CHUNK = 512
HALF = 256
SCALE = HD ** (-0.5) * 1.4426950408889634
LIMIT = 2.0**60
F32 = jnp.float32
BF16 = jnp.bfloat16
VMEM_LIMIT = 56 * 2**20
CUT = 384


def shift(x, axis, size, by):
    return lax.ppermute(x, axis, [(i, (i + by) % size) for i in range(size)])


def exchange(x, by):
    return lax.ppermute(x, ("xhi", "core"), [(i, i ^ by) for i in range(4)])


def normalize(tokens, norm_gain):
    values32 = tokens.astype(F32)
    mean_square = jnp.mean(values32 * values32, axis=-1, keepdims=True)
    return (values32 * lax.rsqrt(mean_square + 1e-05) * norm_gain.astype(F32)).astype(BF16)


def gather_weight(a):
    b = shift(a, "xlo", 2, 1)
    au, ad = shift(a, "y", 4, 1), shift(a, "y", 4, -1)
    a2u, a2d = shift(au[:CUT], "y", 4, 1), shift(ad[CUT:], "y", 4, -1)
    bu, bd = shift(b, "y", 4, 1), shift(b, "y", 4, -1)
    b2u, b2d = shift(a2u, "xlo", 2, 1), shift(a2d, "xlo", 2, 1)
    return [a, au, ad, a2u, a2d, b, bu, bd, b2u, b2d]


def project_kernel(at_ref, own_ref, partner_ref, *refs):
    pieces, (mine_ref, away_ref, weight) = refs[:10], refs[10:]
    for index, piece in enumerate(pieces):
        rows = piece.shape[0]
        weight[pl.ds(pl.multiple_of(at_ref[index], 128), rows), :] = piece[...]
    for part, tokens_ref in enumerate((own_ref, partner_ref)):
        rows = jnp.dot(tokens_ref[...], weight[...], preferred_element_type=F32).astype(BF16)
        mine_ref[part * HALF : (part + 1) * HALF, :] = rows[:, :HD]
        away_ref[part * HALF : (part + 1) * HALF, :] = rows[:, HD:]


def project(at, own, partner, pieces):
    depth = own.shape[1]
    vmem = pl.BlockSpec(memory_space=pltpu.VMEM)
    out = jax.ShapeDtypeStruct((2 * HALF, HD), BF16)
    return pl.pallas_call(
        project_kernel,
        out_shape=(out, out),
        in_specs=[pl.BlockSpec(memory_space=pltpu.SMEM)] + [vmem] * 12,
        out_specs=(vmem, vmem),
        scratch_shapes=[pltpu.VMEM((depth, 2 * HD), BF16)],
        compiler_params=pltpu.CompilerParams(vmem_limit_bytes=VMEM_LIMIT),
        cost_estimate=pl.CostEstimate(
            flops=2 * 2 * HALF * depth * 2 * HD, bytes_accessed=8 * 2**20, transcendentals=0
        ),
    )(at, own, partner, *pieces)


def attend_kernel(at_ref, first_ref, second_ref, key_ref, value_ref, out_ref, query, shifts, acc, total):
    prefix, core = at_ref[0], at_ref[1]
    heads = [slice(g * CHUNK, (g + 1) * CHUNK) for g in range(GROUP)]
    for g in range(GROUP):
        query[g * CHUNK : g * CHUNK + HALF, :] = first_ref[:, g * HD : (g + 1) * HD]
        query[g * CHUNK + HALF : (g + 1) * CHUNK, :] = second_ref[:, g * HD : (g + 1) * HD]

    def block(ref, index):
        start = lax.rem(index, 8) * (2 * CHUNK) + lax.div(index, 8) * CHUNK
        return ref[pl.ds(pl.multiple_of(start, CHUNK), CHUNK), :]

    def score(rows, keys):
        return SCALE * lax.dot_general(
            query[rows, :], keys, (((1,), (1,)), ((), ())), preferred_element_type=F32
        )

    def lanes(x):
        return [x[:, j : j + HD] for j in range(0, x.shape[1], HD)]

    def masked(x):
        row = (lax.broadcasted_iota(jnp.int32, x.shape, 0) + core * HALF) & (CHUNK - 1)
        col = (lax.broadcasted_iota(jnp.int32, x.shape, 1) + core * HALF) & (CHUNK - 1)
        return jnp.where(col <= row, x, -1e30)

    def largest(x):
        top = functools.reduce(jnp.maximum, lanes(x))
        return jnp.broadcast_to(jnp.max(top, axis=1, keepdims=True), top.shape)

    def weigh(x, top, values):
        parts = [jnp.exp2(part - top) for part in lanes(x)]
        low = jnp.concatenate([part.astype(BF16) for part in parts], axis=1)
        return functools.reduce(jnp.add, parts), jnp.dot(low, values, preferred_element_type=F32)

    def diagonal():
        keys, values = block(key_ref, prefix), block(value_ref, prefix)
        for rows in heads:
            scores = masked(score(rows, keys))
            top = largest(scores)
            shifts[rows, :] = top
            total[rows, :], acc[rows, :] = weigh(scores, top, values)

    def plain(keys, values):
        for rows in heads:
            added, update = weigh(score(rows, keys), shifts[rows, :], values)
            total[rows, :] += added
            acc[rows, :] += update

    def pair(index, carry):
        keys = jnp.concatenate([block(key_ref, 2 * index), block(key_ref, 2 * index + 1)], axis=0)
        values = jnp.concatenate(
            [block(value_ref, 2 * index), block(value_ref, 2 * index + 1)], axis=0
        )
        plain(keys, values)
        return carry

    def single(index, carry):
        plain(block(key_ref, index), block(value_ref, index))
        return carry

    def online(index, carry):
        keys, values = block(key_ref, index), block(value_ref, index)
        for rows in heads:
            scores = score(rows, keys)
            before = shifts[rows, :]
            top = jnp.maximum(before, largest(scores))
            factor = jnp.exp2(before - top)
            added, update = weigh(scores, top, values)
            shifts[rows, :] = top
            total[rows, :] = total[rows, :] * factor + added
            acc[rows, :] = acc[rows, :] * factor + update
        return carry

    diagonal()
    pairs = lax.div(prefix, 2)
    lax.fori_loop(0, pairs, pair, 0)
    lax.fori_loop(2 * pairs, prefix, single, 0)

    @pl.when(jnp.logical_not(jnp.max(total[...]) < LIMIT))
    def _():
        diagonal()
        lax.fori_loop(0, prefix, online, 0)

    for g, rows in enumerate(heads):
        summed = jnp.sum(total[rows, :], axis=1, keepdims=True)
        out_ref[:, g * HD : (g + 1) * HD] = (acc[rows, :] / summed).astype(BF16)


def attend(prefix, core, first, second, keys, values):
    vmem = pl.BlockSpec(memory_space=pltpu.VMEM)
    rows = GROUP * CHUNK
    return pl.pallas_call(
        attend_kernel,
        out_shape=jax.ShapeDtypeStruct((CHUNK, GROUP * HD), BF16),
        in_specs=[pl.BlockSpec(memory_space=pltpu.SMEM)] + [vmem] * 4,
        out_specs=vmem,
        scratch_shapes=[
            pltpu.VMEM((rows, HD), BF16),
            pltpu.VMEM((rows, HD), F32),
            pltpu.VMEM((rows, HD), F32),
            pltpu.VMEM((rows, HD), F32),
        ],
        compiler_params=pltpu.CompilerParams(vmem_limit_bytes=VMEM_LIMIT),
        cost_estimate=pl.CostEstimate(
            flops=4 * rows * 8 * CHUNK * HD, bytes_accessed=6 * 2**20, transcendentals=0
        ),
    )(jnp.stack([prefix, core]), first, second, keys, values)


def assemble_kernel(index_ref, *refs):
    pieces, out_ref = refs[:4], refs[4]
    width = pieces[0].shape[1]
    for by in range(4):
        at = pl.multiple_of((index_ref[0] ^ by) * width, 128)
        out_ref[:, pl.ds(at, width)] = pieces[by][...]


def assemble(index, pieces):
    vmem = pl.BlockSpec(memory_space=pltpu.VMEM)
    rows, width = pieces[0].shape
    return pl.pallas_call(
        assemble_kernel,
        out_shape=jax.ShapeDtypeStruct((rows, 4 * width), BF16),
        in_specs=[pl.BlockSpec(memory_space=pltpu.SMEM)] + [vmem] * 4,
        out_specs=vmem,
        compiler_params=pltpu.CompilerParams(vmem_limit_bytes=VMEM_LIMIT),
    )(index[None], *pieces)


def local(tokens, queries, norm_gain, key_weight, value_weight):
    y, xlo = lax.axis_index("y"), lax.axis_index("xlo")
    xhi, z, core = lax.axis_index("xhi"), lax.axis_index("z"), lax.axis_index("core")
    index = 2 * xhi + core

    def columns(weight):
        cut = lambda head: lax.dynamic_slice_in_dim(weight, head * HD, HD, 1)
        return jnp.concatenate([cut(index), cut(index ^ 2)], axis=1)

    key_pieces = gather_weight(columns(key_weight))
    value_pieces = gather_weight(columns(value_weight))
    own = normalize(tokens[0], norm_gain)
    partner = exchange(own, 1)

    shard = key_weight.shape[0]
    turn = lambda by: ((y + by) & 3) * 2
    at = jnp.stack(
        [
            (turn(by) + side) * shard + more
            for side in (xlo, 1 - xlo)
            for by, more in ((0, 0), (3, 0), (1, 0), (2, 0), (2, CUT))
        ]
    )

    def spread(pieces):
        mine, away = project(at, own, partner, pieces)
        other = exchange(away, 2)
        pair = jnp.concatenate(
            [jnp.where(xhi == 0, mine, other), jnp.where(xhi == 0, other, mine)], axis=0
        )
        return lax.all_gather(pair, "z", axis=0, tiled=True)

    width = GROUP * HD
    cut = lambda by: lax.dynamic_slice_in_dim(queries[0], (index ^ by) * width, width, 1)
    asked = [cut(0)] + [exchange(cut(by), by) for by in (1, 2, 3)]

    keys = spread(key_pieces)
    values = spread(value_pieces)
    away = attend((1 - xhi) * 8 + z, core, asked[2], asked[3], keys, values)
    third, second = exchange(away[:HALF], 2), exchange(away[HALF:], 3)
    mine = attend(xhi * 8 + z, core, asked[0], asked[1], keys, values)
    first = exchange(mine[HALF:], 1)
    return assemble(index, [mine[:HALF], first, third, second])[None]


def solution(mesh):
    fine = Mesh(mesh.devices.reshape(4, 2, 2, 8, 2), ("y", "xlo", "xhi", "z", "core"))
    dp, ctx = ("y", "xlo"), ("xhi", "z", "core")
    in_specs = (P(dp, ctx, None), P(dp, ctx, None), P(), P(dp, None), P(dp, None))
    return jax.shard_map(
        local, mesh=fine, in_specs=in_specs, out_specs=P(dp, ctx, None), check_vma=False
    )
```

```python
import functools

import jax
import jax.numpy as jnp
from jax import lax
from jax.experimental import pallas as pl
from jax.experimental.pallas import tpu as pltpu
from jax.sharding import Mesh
from jax.sharding import PartitionSpec as P

GROUP = 5
HD = 128
CHUNK = 512
HALF = 256
BLOCK = 2 * CHUNK
SCALE = HD ** (-0.5) * 1.4426950408889634
LIMIT = 2.0**60
F32 = jnp.float32
BF16 = jnp.bfloat16
VMEM_LIMIT = 20 * 2**20
ATTEND_VMEM = 28 * 2**20
SPANS = ((0, 1, 2, 3, 4),)
CUT = 384
LOW, HIGH = slice(0, CHUNK), slice(CHUNK, BLOCK)


def shift(x, axis, size, by):
    return lax.ppermute(x, axis, [(i, (i + by) % size) for i in range(size)])


def exchange(x, by):
    return lax.ppermute(x, ("xhi", "core"), [(i, i ^ by) for i in range(4)])


def normalize(tokens, norm_gain):
    values32 = tokens.astype(F32)
    mean_square = jnp.mean(values32 * values32, axis=-1, keepdims=True)
    return (values32 * lax.rsqrt(mean_square + 1e-05) * norm_gain.astype(F32)).astype(BF16)


def group_index():
    return 2 * lax.axis_index("xhi") + lax.axis_index("core")


def aligned(start, size):
    return pl.ds(pl.multiple_of(start, 128), size)


def whole(count):
    return [pl.BlockSpec(memory_space=pltpu.VMEM)] * count


def columns_kernel(key_ref, value_ref, out_ref, done):
    index = group_index()
    copies = [
        pltpu.make_async_copy(
            ref.at[:, aligned((index ^ (2 * part)) * HD, HD)],
            out_ref.at[:, (2 * part + number) * HD : (2 * part + number + 1) * HD],
            done.at[2 * part + number],
        )
        for part in range(2)
        for number, ref in enumerate((key_ref, value_ref))
    ]
    for copy in copies:
        copy.start()
    for copy in copies:
        copy.wait()


def columns(key_weight, value_weight):
    return pl.pallas_call(
        columns_kernel,
        out_shape=jax.ShapeDtypeStruct((key_weight.shape[0], 4 * HD), BF16),
        in_specs=[pl.BlockSpec(memory_space=pl.ANY)] * 2,
        out_specs=whole(1)[0],
        scratch_shapes=[pltpu.SemaphoreType.DMA((4,))],
        compiler_params=pltpu.CompilerParams(vmem_limit_bytes=VMEM_LIMIT),
    )(key_weight, value_weight)


def split_kernel(whole_ref, *outs):
    index, width = group_index(), outs[0].shape[1]
    for by, out_ref in enumerate(outs):
        out_ref[...] = whole_ref[:, aligned((index ^ by) * width, width)]


def split(queries):
    rows, width = queries.shape[0], queries.shape[1] // 4
    return pl.pallas_call(
        split_kernel,
        out_shape=(jax.ShapeDtypeStruct((rows, width), BF16),) * 4,
        in_specs=whole(1),
        out_specs=tuple(whole(4)),
        compiler_params=pltpu.CompilerParams(vmem_limit_bytes=VMEM_LIMIT),
    )(queries)


def project_kernel(side, own_ref, partner_ref, *refs):
    pieces, refs = refs[:5], refs[5:]
    y, xlo = lax.axis_index("y"), lax.axis_index("xlo")
    shard = pieces[0].shape[0]
    sums = refs[0] if side == 0 else refs[-1]
    if side == 1:
        sums[...] = refs[0][...]
    for index, (by, more) in enumerate(((0, 0), (3, 0), (1, 0), (2, 0), (2, CUT))):
        piece = pieces[index]
        columns_here = aligned((((y + by) & 3) * 2 + (xlo ^ side)) * shard + more, piece.shape[0])
        for part, tokens_ref in enumerate((own_ref, partner_ref)):
            rows = slice(part * HALF, (part + 1) * HALF)
            update = jnp.dot(tokens_ref[:, columns_here], piece[...], preferred_element_type=F32)
            sums[rows, :] = update if side == 0 and index == 0 else sums[rows, :] + update
    if side == 1:
        refs[1][...] = sums[:, : 2 * HD].astype(BF16)
        refs[2][...] = sums[:, 2 * HD :].astype(BF16)


def project(side, own, partner, pieces, sums=()):
    depth = own.shape[1]
    done = jax.ShapeDtypeStruct((2 * HALF, 2 * HD), BF16)
    partial = jax.ShapeDtypeStruct((2 * HALF, 4 * HD), F32)
    return pl.pallas_call(
        functools.partial(project_kernel, side),
        out_shape=partial if side == 0 else (done, done),
        in_specs=whole(7 + len(sums)),
        out_specs=whole(1)[0] if side == 0 else tuple(whole(2)),
        scratch_shapes=[] if side == 0 else [pltpu.VMEM(partial.shape, F32)],
        compiler_params=pltpu.CompilerParams(vmem_limit_bytes=VMEM_LIMIT),
        cost_estimate=pl.CostEstimate(
            flops=2 * HALF * depth * 4 * HD, bytes_accessed=9 * 2**20, transcendentals=0
        ),
    )(own, partner, *pieces, *sums)


def lanes(x):
    return [x[:, j : j + HD] for j in range(0, x.shape[1], HD)]


def widen(column):
    return jnp.broadcast_to(column, (column.shape[0], HD))


def largest(x):
    return widen(jnp.max(functools.reduce(jnp.maximum, lanes(x)), axis=1, keepdims=True))


def tile(head, half):
    start = head * BLOCK + half * CHUNK
    return pl.ds(start if isinstance(start, int) else pl.multiple_of(start, CHUNK), CHUNK)


def score(query, rows, keys):
    return SCALE * lax.dot_general(
        query[rows, :], keys, (((1,), (1,)), ((), ())), preferred_element_type=F32
    )


def weigh(x, top, values):
    exps = [jnp.exp2(part - top) for part in lanes(x)]
    low = jnp.concatenate([part.astype(BF16) for part in exps], axis=1)
    return functools.reduce(jnp.add, exps), jnp.dot(low, values, preferred_element_type=F32)


def diagonal(query, rows, block, span, core, to, state):
    acc, total, shifts = state
    scores = score(query, rows, block[span, :HD])
    place = lambda axis: (lax.broadcasted_iota(jnp.int32, scores.shape, axis) + core * HALF) & (
        CHUNK - 1
    )
    scores = jnp.where(place(1) <= place(0), scores, -1e30)
    top = largest(scores)
    shifts[to, :] = top
    total[to, :], acc[to, :] = weigh(scores, top, block[span, HD:])


def plain(query, rows, block, span, top, to, state):
    acc, total = state
    added, update = weigh(score(query, rows, block[span, :HD]), top, block[span, HD:])
    total[to, :] += added
    acc[to, :] += update


def online(query, rows, block, span, to, state):
    acc, total, shifts = state
    scores = score(query, rows, block[span, :HD])
    before = shifts[to, :]
    top = jnp.maximum(before, largest(scores))
    factor = jnp.exp2(before - top)
    added, update = weigh(scores, top, block[span, HD:])
    shifts[to, :] = top
    total[to, :] = total[to, :] * factor + added
    acc[to, :] = acc[to, :] * factor + update


def visit(place, z, heads, absorb):
    @pl.when(place < z)
    def _():
        for head in heads:
            absorb(head, 1, slice(0, BLOCK))
            absorb(head, 0, LOW)

    @pl.when(place > z)
    def _():
        for head in heads:
            absorb(head, 1, LOW)


def open_kernel(*refs):
    asked, block, query, acc, total, shifts = refs[:4], *refs[4:]
    xhi, core = lax.axis_index("xhi"), lax.axis_index("core")
    for number, ref in enumerate(asked):
        at = ((number // 2) ^ xhi) * CHUNK + (number % 2) * HALF
        for head in range(GROUP):
            query[aligned(head * BLOCK + at, HALF), :] = ref[:, head * HD : (head + 1) * HD]
    for head in range(GROUP):
        for half, span in enumerate((LOW, HIGH)):
            rows = tile(head, half)
            diagonal(query, rows, block, span, core, rows, (acc, total, shifts))
    for head in range(GROUP):
        rows = tile(head, 1)
        plain(query, rows, block, LOW, shifts[rows, :], rows, (acc, total))


def step_kernel(step, query, shifts, acc_in, total_in, up, down, acc, total, held):
    z = lax.axis_index("z")
    held[0], held[1] = up[...], down[...]
    acc[...], total[...] = acc_in[...], total_in[...]

    def one_block(number, carry):
        block = held.at[number]
        place = (z + jnp.where(number == 0, -step, step)) & 7

        def absorb(head, half, span):
            rows = tile(head, half)
            plain(query, rows, block, span, shifts[rows, :], rows, (acc, total))

        visit(place, z, range(GROUP), absorb)
        return carry

    lax.fori_loop(0, 2, one_block, 0)


def close_kernel(heads, *refs):
    query, shifts, acc_in, total_in, across_low, across_high = refs[:6]
    far, refs = refs[6:13], refs[13:]
    outs, (acc, total, tops, result, held, again, done) = refs[:4], refs[4:]
    xhi, z, core = lax.axis_index("xhi"), lax.axis_index("z"), lax.axis_index("core")
    held[LOW, :], held[HIGH, :] = across_low[...], across_high[...]
    start = pl.ds(heads[0] * BLOCK, len(heads) * BLOCK)
    acc[...], total[...] = acc_in[start, :], total_in[start, :]

    def last(head, half, span):
        rows, to = tile(head, half), tile(head - heads[0], half)
        plain(query, rows, held, span, shifts[rows, :], to, (acc, total))

    visit((z + 4) & 7, z, heads, last)

    @pl.when(jnp.logical_not(jnp.max(total[...]) < LIMIT))
    def _():
        state = (acc, total, tops)

        def bring(ref):
            copy = pltpu.make_async_copy(ref, again, done)
            copy.start()
            copy.wait()

        def each_head(work):
            lax.fori_loop(heads[0], heads[-1] + 1, lambda head, carry: (work(head), carry)[1], 0)

        def redo(block, place):
            def absorb(head, half, span):
                online(query, tile(head, half), block, span, tile(head - heads[0], half), state)

            each_head(lambda head: visit(place, z, (head,), absorb))

        def own(head):
            for half, span in enumerate((LOW, HIGH)):
                to = tile(head - heads[0], half)
                diagonal(query, tile(head, half), again, span, core, to, state)
            online(query, tile(head, 1), again, LOW, tile(head - heads[0], 1), state)

        bring(far[0])
        each_head(own)
        for ref, by in zip(far[1:], (-1, 1, -2, 2, -3, 3)):
            bring(ref)
            redo(again, (z + by) & 7)
        redo(held, (z + 4) & 7)

    ones = jnp.ones((3 * HD, HD), BF16)
    for number in range(len(heads)):
        for half in range(2):
            rows = tile(number, half)
            rest, parts = total[rows, :], []
            for _ in range(3):
                parts.append(rest.astype(BF16))
                rest = rest - parts[-1].astype(F32)
            summed = jnp.dot(jnp.concatenate(parts, axis=1), ones, preferred_element_type=F32)
            result[rows, :] = (acc[rows, :] / summed).astype(BF16)
        for part, out_ref in enumerate(outs):
            side = xhi if part < 2 else 1 - xhi
            at = number * BLOCK + side * CHUNK + (part % 2) * HALF
            out_ref[:, number * HD : (number + 1) * HD] = result[aligned(at, HALF), :]


def attend(kernel, operands, far, out_shape, scratch):
    return pl.pallas_call(
        kernel,
        out_shape=tuple(out_shape),
        in_specs=whole(len(operands)) + [pl.BlockSpec(memory_space=pl.ANY)] * len(far),
        out_specs=tuple(whole(len(out_shape))),
        scratch_shapes=scratch,
        compiler_params=pltpu.CompilerParams(vmem_limit_bytes=ATTEND_VMEM),
        cost_estimate=pl.CostEstimate(
            flops=8 * GROUP * BLOCK * BLOCK * HD, bytes_accessed=8 * 2**20, transcendentals=0
        ),
    )(*operands, *far)


def assemble_kernel(spans, *refs):
    pieces, out_ref = refs[:-1], refs[-1]
    index, width = group_index(), out_ref.shape[1] // 4
    for number, piece in enumerate(pieces):
        by, span = number % 4, spans[number // 4]
        at = (index ^ by) * width + span[0] * HD
        out_ref[:, aligned(at, len(span) * HD)] = piece[...]


def assemble(spans, pieces):
    return pl.pallas_call(
        functools.partial(assemble_kernel, spans),
        out_shape=jax.ShapeDtypeStruct((HALF, 4 * GROUP * HD), BF16),
        in_specs=whole(len(pieces)),
        out_specs=whole(1)[0],
        compiler_params=pltpu.CompilerParams(vmem_limit_bytes=VMEM_LIMIT),
    )(*pieces)


def attention(asked, block):
    rows = GROUP * BLOCK
    state_shape = [jax.ShapeDtypeStruct((rows, HD), F32)] * 2
    query, *state, shifts = attend(
        open_kernel,
        [*asked, block],
        [],
        [jax.ShapeDtypeStruct((rows, HD), BF16)] + state_shape + state_shape[:1],
        [],
    )
    up, down = block, block
    blocks = [block]
    for step in (1, 2, 3):
        up, down = shift(up, "z", 8, 1), shift(down, "z", 8, -1)
        up, down, state = lax.optimization_barrier((up, down, state))
        blocks += [up, down]
        if step == 3:
            across = [shift(up[:CHUNK], "z", 8, 1), shift(down[CHUNK:], "z", 8, -1)]
        state = attend(
            functools.partial(step_kernel, step),
            [query, shifts, *state, up, down],
            [],
            state_shape,
            [pltpu.VMEM((2, BLOCK, 2 * HD), BF16)],
        )
    across, state = lax.optimization_barrier((across, state))
    pieces = []
    for heads in SPANS:
        mine = len(heads) * BLOCK
        out = attend(
            functools.partial(close_kernel, heads),
            [query, shifts, *state, *across],
            blocks,
            [jax.ShapeDtypeStruct((HALF, len(heads) * HD), BF16)] * 4,
            [pltpu.VMEM((mine, HD), F32)] * 3
            + [pltpu.VMEM((mine, HD), BF16)]
            + [pltpu.VMEM((BLOCK, 2 * HD), BF16)] * 2
            + [pltpu.SemaphoreType.DMA],
        )
        out, state = lax.optimization_barrier((out, state))
        if pieces:
            out, pieces = lax.optimization_barrier((out, pieces))
        pieces = [*pieces, out[0]] + [exchange(out[by], by) for by in (1, 2, 3)]
    return assemble(SPANS, pieces)


def local(tokens, queries, norm_gain, key_weight, value_weight):
    near = lax.axis_index("xhi") == 0
    a = columns(key_weight, value_weight)
    b = shift(a, "xlo", 2, 1)
    au, ad = shift(a, "y", 4, 1), shift(a, "y", 4, -1)
    own = normalize(tokens[0], norm_gain)
    asked = split(queries[0])
    b, au, ad, own, asked = lax.optimization_barrier((b, au, ad, own, asked))
    partner = exchange(own, 1)
    asked = [asked[0]] + [exchange(asked[by], by) for by in (1, 2, 3)]
    a2u, a2d = shift(au[:CUT], "y", 4, 1), shift(ad[CUT:], "y", 4, -1)
    b, a2u, a2d, asked, partner = lax.optimization_barrier((b, a2u, a2d, asked, partner))
    bu, bd = shift(b, "y", 4, 1), shift(b, "y", 4, -1)
    b2u, b2d = shift(a2u, "xlo", 2, 1), shift(a2d, "xlo", 2, 1)
    sums = project(0, own, partner, [a, au, ad, a2u, a2d])
    bu, bd, b2u, b2d, sums = lax.optimization_barrier((bu, bd, b2u, b2d, sums))
    mine, away = project(1, own, partner, [b, bu, bd, b2u, b2d], [sums])
    other = exchange(away, 2)
    block = jnp.concatenate([jnp.where(near, mine, other), jnp.where(near, other, mine)], axis=0)
    return attention(asked, block)[None]


def solution(mesh):
    fine = Mesh(mesh.devices.reshape(4, 2, 2, 8, 2), ("y", "xlo", "xhi", "z", "core"))
    dp, ctx = ("y", "xlo"), ("xhi", "z", "core")
    in_specs = (P(dp, ctx, None), P(dp, ctx, None), P(), P(dp, None), P(dp, None))
    return jax.shard_map(
        local, mesh=fine, in_specs=in_specs, out_specs=P(dp, ctx, None), check_vma=False
    )
```

```python
import functools

import jax
import jax.numpy as jnp
from jax import lax
from jax.experimental import pallas as pl
from jax.experimental.pallas import tpu as pltpu
from jax.sharding import Mesh
from jax.sharding import PartitionSpec as P

GROUP = 5
HD = 128
CHUNK = 512
HALF = 256
BLOCK = 2 * CHUNK
SCALE = HD ** (-0.5) * 1.4426950408889634
LIMIT = 2.0**60
F32 = jnp.float32
BF16 = jnp.bfloat16
VMEM_LIMIT = 20 * 2**20
ATTEND_VMEM = 28 * 2**20
SPANS = ((0, 1, 2), (3, 4))
UNROLL = 5
CUT = 384
LOW, HIGH = slice(0, CHUNK), slice(CHUNK, BLOCK)


def shift(x, axis, size, by):
    return lax.ppermute(x, axis, [(i, (i + by) % size) for i in range(size)])


def exchange(x, by):
    return lax.ppermute(x, ("xhi", "core"), [(i, i ^ by) for i in range(4)])


def normalize(tokens, norm_gain):
    values32 = tokens.astype(F32)
    mean_square = jnp.mean(values32 * values32, axis=-1, keepdims=True)
    return (values32 * lax.rsqrt(mean_square + 1e-05) * norm_gain.astype(F32)).astype(BF16)


def group_index():
    return 2 * lax.axis_index("xhi") + lax.axis_index("core")


def aligned(start, size):
    return pl.ds(pl.multiple_of(start, 128), size)


def whole(count):
    return [pl.BlockSpec(memory_space=pltpu.VMEM)] * count


def columns_kernel(key_ref, value_ref, out_ref, done):
    index = group_index()
    copies = [
        pltpu.make_async_copy(
            ref.at[:, aligned((index ^ (2 * part)) * HD, HD)],
            out_ref.at[:, (2 * part + number) * HD : (2 * part + number + 1) * HD],
            done.at[2 * part + number],
        )
        for part in range(2)
        for number, ref in enumerate((key_ref, value_ref))
    ]
    for copy in copies:
        copy.start()
    for copy in copies:
        copy.wait()


def columns(key_weight, value_weight):
    return pl.pallas_call(
        columns_kernel,
        out_shape=jax.ShapeDtypeStruct((key_weight.shape[0], 4 * HD), BF16),
        in_specs=[pl.BlockSpec(memory_space=pltpu.HBM)] * 2,
        out_specs=whole(1)[0],
        scratch_shapes=[pltpu.SemaphoreType.DMA((4,))],
        compiler_params=pltpu.CompilerParams(vmem_limit_bytes=VMEM_LIMIT),
    )(key_weight, value_weight)


def split_kernel(whole_ref, *outs):
    index, width = group_index(), outs[0].shape[1]
    for by, out_ref in enumerate(outs):
        out_ref[...] = whole_ref[:, aligned((index ^ by) * width, width)]


def split(queries):
    rows, width = queries.shape[0], queries.shape[1] // 4
    return pl.pallas_call(
        split_kernel,
        out_shape=(jax.ShapeDtypeStruct((rows, width), BF16),) * 4,
        in_specs=whole(1),
        out_specs=tuple(whole(4)),
        compiler_params=pltpu.CompilerParams(vmem_limit_bytes=VMEM_LIMIT),
    )(queries)


def project_kernel(side, own_ref, partner_ref, *refs):
    pieces, refs = refs[:5], refs[5:]
    y, xlo = lax.axis_index("y"), lax.axis_index("xlo")
    shard = pieces[0].shape[0]
    sums = refs[0] if side == 0 else refs[-1]
    if side == 1:
        sums[...] = refs[0][...]
    for index, (by, more) in enumerate(((0, 0), (3, 0), (1, 0), (2, 0), (2, CUT))):
        piece = pieces[index]
        columns_here = aligned((((y + by) & 3) * 2 + (xlo ^ side)) * shard + more, piece.shape[0])
        for part, tokens_ref in enumerate((own_ref, partner_ref)):
            rows = slice(part * HALF, (part + 1) * HALF)
            update = jnp.dot(tokens_ref[:, columns_here], piece[...], preferred_element_type=F32)
            sums[rows, :] = update if side == 0 and index == 0 else sums[rows, :] + update
    if side == 1:
        refs[1][...] = sums[:, : 2 * HD].astype(BF16)
        refs[2][...] = sums[:, 2 * HD :].astype(BF16)


def project(side, own, partner, pieces, sums=()):
    depth = own.shape[1]
    done = jax.ShapeDtypeStruct((2 * HALF, 2 * HD), BF16)
    partial = jax.ShapeDtypeStruct((2 * HALF, 4 * HD), F32)
    return pl.pallas_call(
        functools.partial(project_kernel, side),
        out_shape=partial if side == 0 else (done, done),
        in_specs=whole(7 + len(sums)),
        out_specs=whole(1)[0] if side == 0 else tuple(whole(2)),
        scratch_shapes=[] if side == 0 else [pltpu.VMEM(partial.shape, F32)],
        compiler_params=pltpu.CompilerParams(vmem_limit_bytes=VMEM_LIMIT),
        cost_estimate=pl.CostEstimate(
            flops=2 * HALF * depth * 4 * HD, bytes_accessed=9 * 2**20, transcendentals=0
        ),
    )(own, partner, *pieces, *sums)


def lanes(x):
    return [x[:, j : j + HD] for j in range(0, x.shape[1], HD)]


def widen(column):
    return jnp.broadcast_to(column, (column.shape[0], HD))


def largest(x):
    return widen(jnp.max(functools.reduce(jnp.maximum, lanes(x)), axis=1, keepdims=True))


def tile(head, half):
    start = head * BLOCK + half * CHUNK
    return pl.ds(start if isinstance(start, int) else pl.multiple_of(start, CHUNK), CHUNK)


def score(query, rows, keys):
    return SCALE * lax.dot_general(
        query[rows, :], keys, (((1,), (1,)), ((), ())), preferred_element_type=F32
    )


def weigh(x, top, values):
    exps = [jnp.exp2(part - top) for part in lanes(x)]
    low = jnp.concatenate([part.astype(BF16) for part in exps], axis=1)
    beside = jnp.concatenate([values, jnp.ones_like(values)], axis=1)
    both = jnp.dot(low, beside, preferred_element_type=F32)
    return both[:, HD:], both[:, :HD]


def diagonal(query, rows, block, span, core, to, state):
    acc, total, shifts = state
    scores = score(query, rows, block[span, :HD])
    place = lambda axis: (lax.broadcasted_iota(jnp.int32, scores.shape, axis) + core * HALF) & (
        CHUNK - 1
    )
    scores = jnp.where(place(1) <= place(0), scores, -1e30)
    top = largest(scores)
    shifts[to, :] = top
    total[to, :], acc[to, :] = weigh(scores, top, block[span, HD:])


def plain(query, rows, block, span, top, to, state):
    acc, total = state
    added, update = weigh(score(query, rows, block[span, :HD]), top, block[span, HD:])
    total[to, :] += added
    acc[to, :] += update


def online(query, rows, block, span, to, state):
    acc, total, shifts = state
    scores = score(query, rows, block[span, :HD])
    before = shifts[to, :]
    top = jnp.maximum(before, largest(scores))
    factor = jnp.exp2(before - top)
    added, update = weigh(scores, top, block[span, HD:])
    shifts[to, :] = top
    total[to, :] = total[to, :] * factor + added
    acc[to, :] = acc[to, :] * factor + update


def each(heads, work):
    if len(heads) > UNROLL:
        lax.fori_loop(heads[0], heads[-1] + 1, lambda head, carry: (work(head), carry)[1], 0)
    else:
        for head in heads:
            work(head)


def visit(place, z, heads, absorb):
    def both(head):
        absorb(head, 1, slice(0, BLOCK))
        absorb(head, 0, LOW)

    @pl.when(place < z)
    def _():
        each(heads, both)

    @pl.when(place > z)
    def _():
        each(heads, lambda head: absorb(head, 1, LOW))


def open_kernel(*refs):
    asked, block, query, acc, total, shifts = refs[:4], *refs[4:]
    xhi, core = lax.axis_index("xhi"), lax.axis_index("core")
    for number, ref in enumerate(asked):
        at = ((number // 2) ^ xhi) * CHUNK + (number % 2) * HALF
        for head in range(GROUP):
            query[aligned(head * BLOCK + at, HALF), :] = ref[:, head * HD : (head + 1) * HD]

    def own(head):
        for half, span in enumerate((LOW, HIGH)):
            rows = tile(head, half)
            diagonal(query, rows, block, span, core, rows, (acc, total, shifts))
        rows = tile(head, 1)
        plain(query, rows, block, LOW, shifts[rows, :], rows, (acc, total))

    each(range(GROUP), own)


def step_kernel(step, heads, query, shifts, acc_in, total_in, up, down, acc, total, held):
    z = lax.axis_index("z")
    held[0], held[1] = up[...], down[...]
    start = pl.ds(heads[0] * BLOCK, len(heads) * BLOCK)
    acc[...], total[...] = acc_in[start, :], total_in[start, :]

    def one_block(number, carry):
        block = held.at[number]
        place = (z + jnp.where(number == 0, -step, step)) & 7

        def absorb(head, half, span):
            rows, to = tile(head, half), tile(head - heads[0], half)
            plain(query, rows, block, span, shifts[rows, :], to, (acc, total))

        visit(place, z, heads, absorb)
        return carry

    lax.fori_loop(0, 2, one_block, 0)


def close_kernel(heads, blocks_left, *refs):
    query, shifts, acc_in, total_in, *left = refs[: 4 + blocks_left + 1]
    far, refs = refs[5 + blocks_left : 13], refs[13:]
    outs, (acc, total, tops, result, held, again, done) = refs[:4], refs[4:]
    xhi, z, core = lax.axis_index("xhi"), lax.axis_index("z"), lax.axis_index("core")
    for number, ref in enumerate(left[:-2]):
        held[number] = ref[...]
    held[blocks_left - 1, LOW, :], held[blocks_left - 1, HIGH, :] = left[-2][...], left[-1][...]
    start = pl.ds(0 if blocks_left == 1 else heads[0] * BLOCK, len(heads) * BLOCK)
    acc[...], total[...] = acc_in[start, :], total_in[start, :]

    def place_of(number):
        number = number + 3 - blocks_left
        return (z + jnp.where(number == 0, -3, number + 2)) & 7

    def one_block(number, carry):
        def absorb(head, half, span):
            rows, to = tile(head, half), tile(head - heads[0], half)
            plain(query, rows, held.at[number], span, shifts[rows, :], to, (acc, total))

        visit(place_of(number), z, heads, absorb)
        return carry

    lax.fori_loop(0, blocks_left, one_block, 0)

    @pl.when(jnp.logical_not(jnp.max(total[...]) < LIMIT))
    def _():
        state = (acc, total, tops)

        def bring(ref):
            copy = pltpu.make_async_copy(ref, again, done)
            copy.start()
            copy.wait()

        def each_head(work):
            lax.fori_loop(heads[0], heads[-1] + 1, lambda head, carry: (work(head), carry)[1], 0)

        def redo(block, place):
            def absorb(head, half, span):
                online(query, tile(head, half), block, span, tile(head - heads[0], half), state)

            each_head(lambda head: visit(place, z, (head,), absorb))

        def own(head):
            for half, span in enumerate((LOW, HIGH)):
                to = tile(head - heads[0], half)
                diagonal(query, tile(head, half), again, span, core, to, state)
            online(query, tile(head, 1), again, LOW, tile(head - heads[0], 1), state)

        bring(far[0])
        each_head(own)
        for ref, by in zip(far[1:], (-1, 1, -2, 2, -3, 3)):
            bring(ref)
            redo(again, (z + by) & 7)

        def rest(number, carry):
            redo(held.at[number], place_of(number))
            return carry

        lax.fori_loop(0, blocks_left, rest, 0)

    for number in range(len(heads)):
        for half in range(2):
            rows = tile(number, half)
            result[rows, :] = (acc[rows, :] / total[rows, :]).astype(BF16)
    for number in range(len(heads)):
        for part, out_ref in enumerate(outs):
            side = xhi if part < 2 else 1 - xhi
            at = number * BLOCK + side * CHUNK + (part % 2) * HALF
            out_ref[:, number * HD : (number + 1) * HD] = result[aligned(at, HALF), :]


def attend(kernel, operands, far, out_shape, scratch):
    return pl.pallas_call(
        kernel,
        out_shape=tuple(out_shape),
        in_specs=whole(len(operands)) + [pl.BlockSpec(memory_space=pl.ANY)] * len(far),
        out_specs=tuple(whole(len(out_shape))),
        scratch_shapes=scratch,
        compiler_params=pltpu.CompilerParams(vmem_limit_bytes=ATTEND_VMEM),
        cost_estimate=pl.CostEstimate(
            flops=8 * GROUP * BLOCK * BLOCK * HD, bytes_accessed=8 * 2**20, transcendentals=0
        ),
    )(*operands, *far)


def assemble_kernel(spans, *refs):
    pieces, out_ref = refs[:-1], refs[-1]
    index, width = group_index(), out_ref.shape[1] // 4
    for number, piece in enumerate(pieces):
        by, span = number % 4, spans[number // 4]
        at = (index ^ by) * width + span[0] * HD
        out_ref[:, aligned(at, len(span) * HD)] = piece[...]


def assemble(spans, pieces):
    return pl.pallas_call(
        functools.partial(assemble_kernel, spans),
        out_shape=jax.ShapeDtypeStruct((HALF, 4 * GROUP * HD), BF16),
        in_specs=whole(len(pieces)),
        out_specs=whole(1)[0],
        compiler_params=pltpu.CompilerParams(vmem_limit_bytes=VMEM_LIMIT),
    )(*pieces)


def attention(asked, block):
    rows = GROUP * BLOCK
    state_shape = [jax.ShapeDtypeStruct((rows, HD), F32)] * 2
    query, *state, shifts = attend(
        open_kernel,
        [*asked, block],
        [],
        [jax.ShapeDtypeStruct((rows, HD), BF16)] + state_shape + state_shape[:1],
        [],
    )
    up, down = block, block
    blocks = [block]

    def advance(step, heads, state):
        return attend(
            functools.partial(step_kernel, step, heads),
            [query, shifts, *state, up, down],
            [],
            [jax.ShapeDtypeStruct((len(heads) * BLOCK, HD), F32)] * 2,
            [pltpu.VMEM((2, BLOCK, 2 * HD), BF16)],
        )

    for step in (1, 2, 3):
        up, down = shift(up, "z", 8, 1), shift(down, "z", 8, -1)
        up, down, state = lax.optimization_barrier((up, down, state))
        blocks += [up, down]
        if step < 3:
            state = advance(step, range(GROUP), state)
    across = [shift(up[:CHUNK], "z", 8, 1), shift(down[CHUNK:], "z", 8, -1)]
    early = advance(3, SPANS[0], state)
    across, early = lax.optimization_barrier((across, early))

    def close(heads, state, left, past):
        mine = len(heads) * BLOCK
        count = len(left) - 1
        return attend(
            functools.partial(close_kernel, heads, count),
            [query, shifts, *state, *left],
            past,
            [jax.ShapeDtypeStruct((HALF, len(heads) * HD), BF16)] * 4,
            [pltpu.VMEM((mine, HD), F32)] * 3
            + [pltpu.VMEM((mine, HD), BF16)]
            + [pltpu.VMEM((count, BLOCK, 2 * HD), BF16), pltpu.VMEM((BLOCK, 2 * HD), BF16)]
            + [pltpu.SemaphoreType.DMA],
        )

    def deliver(out):
        return [out[0]] + [exchange(out[by], by) for by in (1, 2, 3)]

    first = close(SPANS[0], early, across, blocks)
    first, state = lax.optimization_barrier((first, state))
    second = close(SPANS[1], state, [up, down, *across], blocks[:5])
    first = deliver(first)
    second, first = lax.optimization_barrier((second, first))
    return assemble(SPANS, first + deliver(second))


def local(tokens, queries, norm_gain, key_weight, value_weight):
    near = lax.axis_index("xhi") == 0
    a = columns(key_weight, value_weight)
    b = shift(a, "xlo", 2, 1)
    au, ad = shift(a, "y", 4, 1), shift(a, "y", 4, -1)
    own = normalize(tokens[0], norm_gain)
    asked = split(queries[0])
    b, au, ad, own, asked = lax.optimization_barrier((b, au, ad, own, asked))
    partner = exchange(own, 1)
    same, late = asked[0], asked[3]
    others = [exchange(asked[1], 1), exchange(asked[2], 2)]
    a2u, a2d = shift(au[:CUT], "y", 4, 1), shift(ad[CUT:], "y", 4, -1)
    b, a2u, a2d, others[1], partner = lax.optimization_barrier((b, a2u, a2d, others[1], partner))
    bu, bd = shift(b, "y", 4, 1), shift(b, "y", 4, -1)
    b2u, b2d = shift(a2u, "xlo", 2, 1), shift(a2d, "xlo", 2, 1)
    sums = project(0, own, partner, [a, au, ad, a2u, a2d])
    bu, bd, b2u, b2d, sums, late = lax.optimization_barrier((bu, bd, b2u, b2d, sums, late))
    others.append(exchange(late, 3))
    mine, away = project(1, own, partner, [b, bu, bd, b2u, b2d], [sums])
    other = exchange(away, 2)
    block = jnp.concatenate([jnp.where(near, mine, other), jnp.where(near, other, mine)], axis=0)
    return attention([same, *others], block)[None]


def solution(mesh):
    fine = Mesh(mesh.devices.reshape(4, 2, 2, 8, 2), ("y", "xlo", "xhi", "z", "core"))
    dp, ctx = ("y", "xlo"), ("xhi", "z", "core")
    in_specs = (P(dp, ctx, None), P(dp, ctx, None), P(), P(dp, None), P(dp, None))
    return jax.shard_map(
        local, mesh=fine, in_specs=in_specs, out_specs=P(dp, ctx, None), check_vma=False
    )
```

```python
import functools

import jax
import jax.numpy as jnp
from jax import lax
from jax.experimental import pallas as pl
from jax.experimental.pallas import tpu as pltpu
from jax.sharding import Mesh
from jax.sharding import PartitionSpec as P

GROUP = 5
HD = 128
CHUNK = 512
HALF = 256
BLOCK = 2 * CHUNK
SCALE = HD ** (-0.5) * 1.4426950408889634
LIMIT = 2.0**60
F32 = jnp.float32
BF16 = jnp.bfloat16
VMEM_LIMIT = 20 * 2**20
ATTEND_VMEM = 28 * 2**20
SPANS = ((0, 1, 2), (3, 4))
UNROLL = 5
CUT = 384
LOW, HIGH = slice(0, CHUNK), slice(CHUNK, BLOCK)


def shift(x, axis, size, by):
    return lax.ppermute(x, axis, [(i, (i + by) % size) for i in range(size)])


def exchange(x, by):
    return lax.ppermute(x, ("xhi", "core"), [(i, i ^ by) for i in range(4)])


def normalize(tokens, norm_gain):
    values32 = tokens.astype(F32)
    mean_square = jnp.mean(values32 * values32, axis=-1, keepdims=True)
    return (values32 * lax.rsqrt(mean_square + 1e-05) * norm_gain.astype(F32)).astype(BF16)


def group_index():
    return 2 * lax.axis_index("xhi") + lax.axis_index("core")


def aligned(start, size):
    return pl.ds(pl.multiple_of(start, 128), size)


def whole(count):
    return [pl.BlockSpec(memory_space=pltpu.VMEM)] * count


def columns_kernel(key_ref, value_ref, out_ref, done):
    index = group_index()
    copies = [
        pltpu.make_async_copy(
            ref.at[:, aligned((index ^ (2 * part)) * HD, HD)],
            out_ref.at[:, (2 * part + number) * HD : (2 * part + number + 1) * HD],
            done.at[2 * part + number],
        )
        for part in range(2)
        for number, ref in enumerate((key_ref, value_ref))
    ]
    for copy in copies:
        copy.start()
    for copy in copies:
        copy.wait()


def columns(key_weight, value_weight):
    return pl.pallas_call(
        columns_kernel,
        out_shape=jax.ShapeDtypeStruct((key_weight.shape[0], 4 * HD), BF16),
        in_specs=[pl.BlockSpec(memory_space=pltpu.HBM)] * 2,
        out_specs=whole(1)[0],
        scratch_shapes=[pltpu.SemaphoreType.DMA((4,))],
        compiler_params=pltpu.CompilerParams(vmem_limit_bytes=VMEM_LIMIT),
    )(key_weight, value_weight)


def split_kernel(whole_ref, *outs):
    index, width = group_index(), outs[0].shape[1]
    for by, out_ref in enumerate(outs):
        out_ref[...] = whole_ref[:, aligned((index ^ by) * width, width)]


def split(queries):
    rows, width = queries.shape[0], queries.shape[1] // 4
    return pl.pallas_call(
        split_kernel,
        out_shape=(jax.ShapeDtypeStruct((rows, width), BF16),) * 4,
        in_specs=whole(1),
        out_specs=tuple(whole(4)),
        compiler_params=pltpu.CompilerParams(vmem_limit_bytes=VMEM_LIMIT),
    )(queries)


def project_kernel(side, own_ref, partner_ref, *refs):
    pieces, refs = refs[:5], refs[5:]
    y, xlo = lax.axis_index("y"), lax.axis_index("xlo")
    shard = pieces[0].shape[0]
    sums = refs[0] if side == 0 else refs[-1]
    if side == 1:
        sums[...] = refs[0][...]
    for index, (by, more) in enumerate(((0, 0), (3, 0), (1, 0), (2, 0), (2, CUT))):
        piece = pieces[index]
        columns_here = aligned((((y + by) & 3) * 2 + (xlo ^ side)) * shard + more, piece.shape[0])
        for part, tokens_ref in enumerate((own_ref, partner_ref)):
            rows = slice(part * HALF, (part + 1) * HALF)
            update = jnp.dot(tokens_ref[:, columns_here], piece[...], preferred_element_type=F32)
            sums[rows, :] = update if side == 0 and index == 0 else sums[rows, :] + update
    if side == 1:
        refs[1][...] = sums[:, : 2 * HD].astype(BF16)
        refs[2][...] = sums[:, 2 * HD :].astype(BF16)


def project(side, own, partner, pieces, sums=()):
    depth = own.shape[1]
    done = jax.ShapeDtypeStruct((2 * HALF, 2 * HD), BF16)
    partial = jax.ShapeDtypeStruct((2 * HALF, 4 * HD), F32)
    return pl.pallas_call(
        functools.partial(project_kernel, side),
        out_shape=partial if side == 0 else (done, done),
        in_specs=whole(7 + len(sums)),
        out_specs=whole(1)[0] if side == 0 else tuple(whole(2)),
        scratch_shapes=[] if side == 0 else [pltpu.VMEM(partial.shape, F32)],
        compiler_params=pltpu.CompilerParams(vmem_limit_bytes=VMEM_LIMIT),
        cost_estimate=pl.CostEstimate(
            flops=2 * HALF * depth * 4 * HD, bytes_accessed=9 * 2**20, transcendentals=0
        ),
    )(own, partner, *pieces, *sums)


def lanes(x):
    return [x[:, j : j + HD] for j in range(0, x.shape[1], HD)]


def widen(column):
    return jnp.broadcast_to(column, (column.shape[0], HD))


def largest(x):
    return widen(jnp.max(functools.reduce(jnp.maximum, lanes(x)), axis=1, keepdims=True))


def tile(head, half):
    start = head * BLOCK + half * CHUNK
    return pl.ds(start if isinstance(start, int) else pl.multiple_of(start, CHUNK), CHUNK)


def score(query, rows, keys):
    return SCALE * lax.dot_general(
        query[rows, :], keys, (((1,), (1,)), ((), ())), preferred_element_type=F32
    )


def weigh(x, top, values):
    exps = [jnp.exp2(part - top) for part in lanes(x)]
    low = jnp.concatenate([part.astype(BF16) for part in exps], axis=1)
    beside = jnp.concatenate([values, jnp.ones_like(values)], axis=1)
    both = jnp.dot(low, beside, preferred_element_type=F32)
    return both[:, HD:], both[:, :HD]


def diagonal(query, rows, block, span, core, to, state):
    acc, total, shifts = state
    scores = score(query, rows, block[span, :HD])
    place = lambda axis: (lax.broadcasted_iota(jnp.int32, scores.shape, axis) + core * HALF) & (
        CHUNK - 1
    )
    scores = jnp.where(place(1) <= place(0), scores, -1e30)
    top = largest(scores)
    shifts[to, :] = top
    total[to, :], acc[to, :] = weigh(scores, top, block[span, HD:])


def plain(query, rows, block, span, top, to, state):
    acc, total = state
    added, update = weigh(score(query, rows, block[span, :HD]), top, block[span, HD:])
    total[to, :] += added
    acc[to, :] += update


def online(query, rows, block, span, to, state):
    acc, total, shifts = state
    scores = score(query, rows, block[span, :HD])
    before = shifts[to, :]
    top = jnp.maximum(before, largest(scores))
    factor = jnp.exp2(before - top)
    added, update = weigh(scores, top, block[span, HD:])
    shifts[to, :] = top
    total[to, :] = total[to, :] * factor + added
    acc[to, :] = acc[to, :] * factor + update


def each(heads, work):
    if len(heads) > UNROLL:
        lax.fori_loop(heads[0], heads[-1] + 1, lambda head, carry: (work(head), carry)[1], 0)
    else:
        for head in heads:
            work(head)


def visit(place, z, heads, absorb):
    def both(head):
        absorb(head, 1, slice(0, BLOCK))
        absorb(head, 0, LOW)

    @pl.when(place < z)
    def _():
        each(heads, both)

    @pl.when(place > z)
    def _():
        each(heads, lambda head: absorb(head, 1, LOW))


def open_kernel(*refs):
    asked, block, query, acc, total, shifts = refs[:4], *refs[4:]
    xhi, core = lax.axis_index("xhi"), lax.axis_index("core")
    for number, ref in enumerate(asked):
        at = ((number // 2) ^ xhi) * CHUNK + (number % 2) * HALF
        for head in range(GROUP):
            query[aligned(head * BLOCK + at, HALF), :] = ref[:, head * HD : (head + 1) * HD]

    def own(head):
        for half, span in enumerate((LOW, HIGH)):
            rows = tile(head, half)
            diagonal(query, rows, block, span, core, rows, (acc, total, shifts))
        rows = tile(head, 1)
        plain(query, rows, block, LOW, shifts[rows, :], rows, (acc, total))

    each(range(GROUP), own)


def step_kernel(step, heads, query, shifts, acc_in, total_in, up, down, acc, total, held):
    z = lax.axis_index("z")
    held[0], held[1] = up[...], down[...]
    start = pl.ds(heads[0] * BLOCK, len(heads) * BLOCK)
    acc[...], total[...] = acc_in[start, :], total_in[start, :]

    def one_block(number, carry):
        block = held.at[number]
        place = (z + jnp.where(number == 0, -step, step)) & 7

        def absorb(head, half, span):
            rows, to = tile(head, half), tile(head - heads[0], half)
            plain(query, rows, block, span, shifts[rows, :], to, (acc, total))

        visit(place, z, heads, absorb)
        return carry

    lax.fori_loop(0, 2, one_block, 0)


def close_kernel(heads, blocks_left, *refs):
    query, shifts, acc_in, total_in, *left = refs[: 4 + blocks_left + 1]
    far, refs = refs[5 + blocks_left : 13], refs[13:]
    outs, (acc, total, tops, result, held, again, done) = refs[:4], refs[4:]
    xhi, z, core = lax.axis_index("xhi"), lax.axis_index("z"), lax.axis_index("core")
    for number, ref in enumerate(left[:-2]):
        held[number] = ref[...]
    held[blocks_left - 1, LOW, :], held[blocks_left - 1, HIGH, :] = left[-2][...], left[-1][...]
    start = pl.ds(0 if blocks_left == 1 else heads[0] * BLOCK, len(heads) * BLOCK)
    acc[...], total[...] = acc_in[start, :], total_in[start, :]

    def place_of(number):
        number = number + 3 - blocks_left
        return (z + jnp.where(number == 0, -3, number + 2)) & 7

    def one_block(number, carry):
        def absorb(head, half, span):
            rows, to = tile(head, half), tile(head - heads[0], half)
            plain(query, rows, held.at[number], span, shifts[rows, :], to, (acc, total))

        visit(place_of(number), z, heads, absorb)
        return carry

    lax.fori_loop(0, blocks_left, one_block, 0)

    @pl.when(jnp.logical_not(jnp.max(total[...]) < LIMIT))
    def _():
        state = (acc, total, tops)

        def bring(ref):
            copy = pltpu.make_async_copy(ref, again, done)
            copy.start()
            copy.wait()

        def each_head(work):
            lax.fori_loop(heads[0], heads[-1] + 1, lambda head, carry: (work(head), carry)[1], 0)

        def redo(block, place):
            def absorb(head, half, span):
                online(query, tile(head, half), block, span, tile(head - heads[0], half), state)

            each_head(lambda head: visit(place, z, (head,), absorb))

        def own(head):
            for half, span in enumerate((LOW, HIGH)):
                to = tile(head - heads[0], half)
                diagonal(query, tile(head, half), again, span, core, to, state)
            online(query, tile(head, 1), again, LOW, tile(head - heads[0], 1), state)

        bring(far[0])
        each_head(own)
        for ref, by in zip(far[1:], (-1, 1, -2, 2, -3, 3)):
            bring(ref)
            redo(again, (z + by) & 7)

        def rest(number, carry):
            redo(held.at[number], place_of(number))
            return carry

        lax.fori_loop(0, blocks_left, rest, 0)

    for number in range(len(heads)):
        for half in range(2):
            rows = tile(number, half)
            result[rows, :] = (acc[rows, :] / total[rows, :]).astype(BF16)
    for number in range(len(heads)):
        for part, out_ref in enumerate(outs):
            side = xhi if part < 2 else 1 - xhi
            at = number * BLOCK + side * CHUNK + (part % 2) * HALF
            out_ref[:, number * HD : (number + 1) * HD] = result[aligned(at, HALF), :]


def attend(kernel, operands, far, out_shape, scratch):
    return pl.pallas_call(
        kernel,
        out_shape=tuple(out_shape),
        in_specs=whole(len(operands)) + [pl.BlockSpec(memory_space=pl.ANY)] * len(far),
        out_specs=tuple(whole(len(out_shape))),
        scratch_shapes=scratch,
        compiler_params=pltpu.CompilerParams(vmem_limit_bytes=ATTEND_VMEM),
        cost_estimate=pl.CostEstimate(
            flops=8 * GROUP * BLOCK * BLOCK * HD, bytes_accessed=8 * 2**20, transcendentals=0
        ),
    )(*operands, *far)


def assemble_kernel(spans, *refs):
    pieces, out_ref = refs[:-1], refs[-1]
    index, width = group_index(), out_ref.shape[1] // 4
    for number, piece in enumerate(pieces):
        by, span = number % 4, spans[number // 4]
        at = (index ^ by) * width + span[0] * HD
        out_ref[:, aligned(at, len(span) * HD)] = piece[...]


def assemble(spans, pieces):
    return pl.pallas_call(
        functools.partial(assemble_kernel, spans),
        out_shape=jax.ShapeDtypeStruct((HALF, 4 * GROUP * HD), BF16),
        in_specs=whole(len(pieces)),
        out_specs=whole(1)[0],
        compiler_params=pltpu.CompilerParams(vmem_limit_bytes=VMEM_LIMIT),
    )(*pieces)


def attention(asked, block):
    rows = GROUP * BLOCK
    state_shape = [jax.ShapeDtypeStruct((rows, HD), F32)] * 2
    query, *state, shifts = attend(
        open_kernel,
        [*asked, block],
        [],
        [jax.ShapeDtypeStruct((rows, HD), BF16)] + state_shape + state_shape[:1],
        [],
    )
    up, down = block, block
    blocks = [block]

    def advance(step, heads, state):
        return attend(
            functools.partial(step_kernel, step, heads),
            [query, shifts, *state, up, down],
            [],
            [jax.ShapeDtypeStruct((len(heads) * BLOCK, HD), F32)] * 2,
            [pltpu.VMEM((2, BLOCK, 2 * HD), BF16)],
        )

    for step in (1, 2, 3):
        up, down = shift(up, "z", 8, 1), shift(down, "z", 8, -1)
        up, down, state = lax.optimization_barrier((up, down, state))
        blocks += [up, down]
        if step < 3:
            state = advance(step, range(GROUP), state)
    across = [shift(up[:CHUNK], "z", 8, 1), shift(down[CHUNK:], "z", 8, -1)]
    early = advance(3, SPANS[0], state)
    across, early = lax.optimization_barrier((across, early))

    def close(heads, state, left, past):
        mine = len(heads) * BLOCK
        count = len(left) - 1
        return attend(
            functools.partial(close_kernel, heads, count),
            [query, shifts, *state, *left],
            past,
            [jax.ShapeDtypeStruct((HALF, len(heads) * HD), BF16)] * 4,
            [pltpu.VMEM((mine, HD), F32)] * 3
            + [pltpu.VMEM((mine, HD), BF16)]
            + [pltpu.VMEM((count, BLOCK, 2 * HD), BF16), pltpu.VMEM((BLOCK, 2 * HD), BF16)]
            + [pltpu.SemaphoreType.DMA],
        )

    def deliver(out):
        return [out[0]] + [exchange(out[by], by) for by in (1, 2, 3)]

    first = close(SPANS[0], early, across, blocks)
    first, state = lax.optimization_barrier((first, state))
    second = close(SPANS[1], state, [up, down, *across], blocks[:5])
    first = deliver(first)
    second = list(second)
    second[1], first = lax.optimization_barrier((second[1], first))
    return assemble(SPANS, first + deliver(second))


def local(tokens, queries, norm_gain, key_weight, value_weight):
    near = lax.axis_index("xhi") == 0
    a = columns(key_weight, value_weight)
    b = shift(a, "xlo", 2, 1)
    au, ad = shift(a, "y", 4, 1), shift(a, "y", 4, -1)
    own = normalize(tokens[0], norm_gain)
    asked = split(queries[0])
    b, au, ad, own, asked = lax.optimization_barrier((b, au, ad, own, asked))
    partner = exchange(own, 1)
    same, late = asked[0], asked[3]
    others = [exchange(asked[1], 1), exchange(asked[2], 2)]
    a2u, a2d = shift(au[:CUT], "y", 4, 1), shift(ad[CUT:], "y", 4, -1)
    b, a2u, a2d, others[1], partner = lax.optimization_barrier((b, a2u, a2d, others[1], partner))
    bu, bd = shift(b, "y", 4, 1), shift(b, "y", 4, -1)
    b2u, b2d = shift(a2u, "xlo", 2, 1), shift(a2d, "xlo", 2, 1)
    sums = project(0, own, partner, [a, au, ad, a2u, a2d])
    bu, bd, b2u, b2d, sums, late = lax.optimization_barrier((bu, bd, b2u, b2d, sums, late))
    others.append(exchange(late, 3))
    mine, away = project(1, own, partner, [b, bu, bd, b2u, b2d], [sums])
    other = exchange(away, 2)
    block = jnp.concatenate([jnp.where(near, mine, other), jnp.where(near, other, mine)], axis=0)
    return attention([same, *others], block)[None]


def solution(mesh):
    fine = Mesh(mesh.devices.reshape(4, 2, 2, 8, 2), ("y", "xlo", "xhi", "z", "core"))
    dp, ctx = ("y", "xlo"), ("xhi", "z", "core")
    in_specs = (P(dp, ctx, None), P(dp, ctx, None), P(), P(dp, None), P(dp, None))
    return jax.shard_map(
        local, mesh=fine, in_specs=in_specs, out_specs=P(dp, ctx, None), check_vma=False
    )
```
